32 devices in a mesh: section: 2 (over y), node: 4 (over x, core), local: 4 (over z).
Axes of the slice: x: 2, y: 2, z: 4, core: 2. Of those that a mesh axis runs over, the one named last changes fastest.
Arguments:
- tokens: bfloat16 [2, 96, 7168], P(None, ('section', 'node', 'local')), may hold values from -6 to 6
- norm_gain: float32 [7168], replicated, may hold values from 0.1 to 1.9
- routes: int32 [2, 96, 2], P(None, ('section', 'node', 'local')), may hold values from 0 to 3, all different within a row; in each aligned block of 3 rows (0 to 2, 3 to 5, ..., all dimensions but the last counted through in order) at most 2 rows name the same one
- gate_weight: float32 [2, 96, 2], P(None, ('section', 'node', 'local')), may hold values from 0.25 to 1
- w_gate: bfloat16 [4, 7168, 2048], P('node', None, 'local'), may hold values from -0.0625 to 0.0625
- w_up: bfloat16 [4, 7168, 2048], P('node', None, 'local'), may hold values from -0.0625 to 0.0625
- w_down: bfloat16 [4, 2048, 7168], P('node', 'local'), may hold values from -0.125 to 0.125
Outputs:
- mixed_out: bfloat16 [2, 96, 7168], P(None, ('section', 'node', 'local'))
The draws below stay inside these ranges and needn't reach their ends.
Inputs may be any that keep to these rules, and one draw needn't show every extreme that they name: `routes`: each row names 2 different experts. Among the 3 events of one device in one microbatch (an aligned block of rows), no expert is named more than 2 times, a bound that some block reaches.
All inputs are finite; a program needn't handle non-finite values.
Results may differ from the reference program's by a relative error of at most 0.011.
Values may be sent and summed in bfloat16 or wider, within the bound.
A program may use at most 64 MiB of HBM per device.

```python
import math
import jax
import jax.numpy as jnp
import numpy as np
from jax import lax

D = 7168
FF = 2048
TOP = 2
MICRO = 2
TOK_DEV = 3
EXPERTS = 4
CAP = 2
EVENTS = 96
N_SECTION = 2
N_LOCAL = 4


def levels(key, dims, split, low, high):
    factor_of = 1.0
    for dim, parts in split:
        steps = jax.random.uniform(jax.random.fold_in(jax.random.fold_in(key, 6), dim), (parts,), jnp.float32, low / len(split), high / len(split))
        factor_of = factor_of * jnp.repeat(jnp.exp(steps), dims[dim] // parts).reshape((-1,) + (1,) * (len(dims) - 1 - dim))
    return factor_of


def shared_out(stream_key, own, number, rows, count, top, bound, slope):
    sequence = jax.random.permutation(stream_key, count)
    heavy_load, common = load_shares(count, rows * top, bound, slope, True), load_shares(count, rows * top, bound, slope, False)
    places = jnp.arange(count)

    def named(lengths, rotation):
        used = int((lengths > 0).sum())
        fixed = max(1, used // 4)
        passed = fixed + (places - fixed + rotation * (used - fixed)) % max(1, count - fixed)
        return jnp.zeros((count,), jnp.int32).at[sequence[jnp.where(places < fixed, places, passed)]].set(jnp.asarray(lengths, jnp.int32))

    lengths = jnp.where(number % 4 == 0, named(heavy_load, number // 4), named(common, number - number // 4 - 1))
    mixed = jax.random.permutation(jax.random.fold_in(own, 3), count)
    giver, receiver = mixed[0:count // 2 * 2:2], mixed[1:count // 2 * 2:2]
    slack = jnp.minimum(lengths[giver] - 1, bound - lengths[receiver]) // 2
    slack = jnp.where((giver == sequence[0]) | (receiver == sequence[0]) | (lengths[receiver] == 0), 0, jnp.maximum(slack, 0))
    passed = jax.random.randint(jax.random.fold_in(own, 4), (count // 2,), 0, 1 << 20) % (slack + 1)
    lengths = lengths.at[giver].add(-passed).at[receiver].add(passed)
    labels = jnp.searchsorted(jnp.cumsum(lengths), jnp.arange(rows * top), side="right").astype(jnp.int32)
    grid = labels.reshape(top, rows).T
    grid = grid[jax.random.permutation(jax.random.fold_in(own, 1), rows)]
    rotation = jax.random.randint(jax.random.fold_in(own, 2), (rows, 1), 0, top)
    return jnp.take_along_axis(grid, (jnp.arange(top)[None, :] + rotation) % top, axis=1)


def load_shares(number_of, total, reach, lean, full):
    weights = [(1 << 20) // math.isqrt(grade ** lean) + 1 for grade in range(1, number_of + 1)]
    largest = reach if full else min(reach, max(-(-total // number_of), total * weights[0] // sum(weights)))
    least = 1 if total - largest >= number_of - 1 else 0
    counts, rest = [largest] + [least] * (number_of - 1), total - largest - least * (number_of - 1)
    while rest > 0:
        movable = [i for i in range(1, number_of) if counts[i] < largest] or [i for i in range(1, number_of) if counts[i] < reach]
        mass, remaining = sum([weights[i] for i in movable]), rest
        for i in movable:
            more = min(reach - counts[i], max(1, remaining * weights[i] // mass), rest)
            counts[i] = counts[i] + more
            rest = rest - more
    return np.array(counts)


def gaussian(rng, shape, deviation, reach, cuts=(), held_as=jnp.bfloat16):
    result = deviation * jax.random.normal(rng, shape, jnp.float32)
    if cuts:
        result = result * levels(rng, shape, cuts, -0.22, 0.18)
    return jnp.clip(result, -reach, reach).astype(held_as)


def setup_inputs(seed: int = 0) -> dict:
    streams_of = jax.random.split(jax.random.key(seed), 8)
    tokens = gaussian(streams_of[0], (MICRO, EVENTS, D), 1.0, 6.0, ((1, 32),))
    norm_gain = jnp.clip(1.0 + 0.18 * jax.random.normal(streams_of[1], (D,), jnp.float32), 0.1, 1.9)
    routes_keys = jax.random.split(jax.random.fold_in(streams_of[2], 1), MICRO * EVENTS // TOK_DEV)
    routes_turns = jax.random.permutation(jax.random.fold_in(streams_of[2], 3), MICRO * EVENTS // TOK_DEV)
    routes = jax.vmap(lambda own, number: shared_out(jax.random.fold_in(streams_of[2], 2), own, number, TOK_DEV, EXPERTS, TOP, CAP, 2))(routes_keys, routes_turns).reshape((MICRO, EVENTS, TOP))
    gate_weight = jnp.clip(0.25 + 0.75 * jax.random.uniform(streams_of[3], (MICRO, EVENTS, TOP), jnp.float32) ** levels(streams_of[3], (MICRO, EVENTS, TOP), ((1, 32),), -0.2, 0.2), 0.25, 1.0)
    w_gate = gaussian(streams_of[4], (EXPERTS, D, FF), D ** -0.5, 0.0625, ((0, 4), (2, 4)))
    w_up = gaussian(streams_of[5], (EXPERTS, D, FF), D ** -0.5, 0.0625, ((0, 4), (2, 4)))
    w_down = gaussian(streams_of[6], (EXPERTS, FF, D), FF ** -0.5, 0.125, ((0, 4), (1, 4)))
    return {"tokens": tokens, "norm_gain": norm_gain, "routes": routes, "gate_weight": gate_weight, "w_gate": w_gate, "w_up": w_up, "w_down": w_down}


def reference(tokens, norm_gain, routes, gate_weight, w_gate, w_up, w_down):
    per_section = EVENTS // N_SECTION
    arrived = jnp.roll(tokens.reshape(MICRO, N_SECTION, per_section, D), 1, axis=1).reshape(MICRO * EVENTS, D)
    wide = arrived.astype(jnp.float32)
    mean_square = lax.optimization_barrier(jnp.mean(wide * wide, axis=1, keepdims=True))
    normed = (wide * lax.rsqrt(mean_square + 1e-06) * norm_gain).astype(jnp.bfloat16)
    blocks = MICRO * EVENTS // TOK_DEV
    block_routes = routes.reshape(blocks, TOK_DEV, TOP).astype(jnp.int32)
    block_gates = gate_weight.reshape(blocks, TOK_DEV, TOP).astype(jnp.float32)
    capacity_rows = blocks * CAP
    hid_dev = FF // N_LOCAL
    source_index = jnp.arange(blocks * TOK_DEV, dtype=jnp.int32).reshape(blocks, TOK_DEV)
    block_base = (jnp.arange(blocks, dtype=jnp.int32) * CAP)[:, None]

    def one_expert(expert, mixed_sum):
        chosen = block_routes == expert
        picked = lax.optimization_barrier(jnp.sum(chosen.astype(jnp.int32), axis=2))
        weight = lax.optimization_barrier(jnp.sum(jnp.where(chosen, block_gates, jnp.float32(0.0)), axis=2))
        slot_rank = jnp.cumsum(picked, axis=1).astype(jnp.int32) - 1
        slot = jnp.where(picked > 0, block_base + slot_rank, capacity_rows).astype(jnp.int32)
        slot_source = jnp.zeros((capacity_rows + 1,), jnp.int32).at[slot.reshape(-1)].set(source_index.reshape(-1))
        row_data = normed[slot_source[:capacity_rows]]
        gate_act = jnp.dot(row_data, w_gate[expert], preferred_element_type=jnp.float32)
        up_act = jnp.dot(row_data, w_up[expert], preferred_element_type=jnp.float32)
        hidden = (jax.nn.silu(gate_act) * up_act).astype(jnp.bfloat16)
        hidden_blocks = jnp.swapaxes(hidden.reshape(capacity_rows, N_LOCAL, hid_dev), 0, 1)
        down_blocks = w_down[expert].reshape(N_LOCAL, hid_dev, D)

        def add_block(partial_sum, pair):
            block_hidden, block_down = pair
            product = jnp.dot(block_hidden, block_down, preferred_element_type=jnp.float32).astype(jnp.bfloat16)
            product = lax.optimization_barrier(product)
            return (partial_sum + product.astype(jnp.float32), None)
        summed = lax.scan(add_block, jnp.zeros((capacity_rows, D), jnp.float32), (hidden_blocks, down_blocks))[0]
        expert_out = jnp.concatenate([summed.astype(jnp.bfloat16), jnp.zeros((1, D), jnp.bfloat16)], axis=0)
        taken = expert_out[slot.reshape(-1)].astype(jnp.float32)
        return mixed_sum + weight.reshape(-1, 1) * taken
    mixed_sum = lax.fori_loop(0, EXPERTS, one_expert, jnp.zeros((MICRO * EVENTS, D), jnp.float32))
    mixed_out = (wide + mixed_sum).astype(jnp.bfloat16)
    return mixed_out.reshape(MICRO, EVENTS, D)
```

```python
import functools

import jax
import jax.numpy as jnp
from jax import lax
from jax.experimental import pallas as pl
from jax.experimental.pallas import tpu as pltpu
from jax.sharding import PartitionSpec as P

MESH = pl.DeviceIdType.MESH
BLOCK = 8
LANES = 128


def kernel(
    sections, locals_, chunks,
    tokens, gain, routes, gate_weight, w_gate, w_up, w_down,
    out,
    gate_v, up_v, down_v, wide_rows, normed, rows, gate_acc, up_acc, arrived,
    own_weights, all_weights, parts, core_in, pair_in, sums, local_in,
    load_sem, a_send, a_recv, w1_send, w1_recv, w2_send, w2_recv,
    s1_send, s1_recv, s2_send, s2_recv, r1_send, r1_recv, r2_send, r2_recv, r3_send, r3_recv,
):
    micro, tok, width = tokens.shape
    step = width // chunks
    total = rows.shape[0] * locals_ * BLOCK
    section, node, local = (lax.axis_index(name) for name in ("section", "node", "local"))
    ahead = lax.rem(section + 1, sections)
    behind = lax.rem(section + sections - 1, sections)
    near, far, cross = node ^ 1, node ^ 2, node ^ 3

    def cut(k):
        return pl.ds(pl.multiple_of(k * step, step), step)

    def peer(offset):
        return lax.rem(local + offset, locals_)

    def each(first, last, body):
        lax.fori_loop(first, last, lambda k, c: (body(k), c)[1], 0)

    def send(src, dst, send_sem, recv_sem, to):
        return pltpu.make_async_remote_copy(
            src_ref=src, dst_ref=dst, send_sem=send_sem, recv_sem=recv_sem,
            device_id=to, device_id_type=MESH,
        )

    def gate_load(k):
        return pltpu.make_async_copy(w_gate.at[0, cut(k), :], gate_v.at[cut(k), :], load_sem.at[0, k])

    def up_load(k):
        return pltpu.make_async_copy(w_up.at[0, cut(k), :], up_v.at[cut(k), :], load_sem.at[1, k])

    def down_load(k):
        return pltpu.make_async_copy(w_down.at[0, :, cut(k)], down_v.at[:, cut(k)], load_sem.at[2, k])

    def start_in(k):
        gate_load(k).start()
        up_load(k).start()

    each(0, chunks, start_in)
    each(0, chunks, lambda k: down_load(k).start())

    barrier = pltpu.get_barrier_semaphore()
    for other in range(locals_):
        pl.semaphore_signal(barrier, inc=1, device_id=(behind, node, other), device_id_type=MESH)
    for offset in range(1, locals_):
        pl.semaphore_signal(barrier, inc=1, device_id=(section, node, peer(offset)), device_id_type=MESH)
    for other in (near, far):
        pl.semaphore_signal(barrier, inc=1, device_id=(section, other, local), device_id_type=MESH)

    own_weights[...] = jnp.zeros_like(own_weights)
    lane = lax.broadcasted_iota(jnp.int32, (tok, LANES), 1)
    for m in range(micro):
        spread = jnp.zeros((tok, LANES), jnp.float32)
        for t in range(routes.shape[2]):
            spread += jnp.where(routes[m, :, t:t + 1] == lane, gate_weight[m, :, t:t + 1], 0.0)
        own_weights[m * tok:(m + 1) * tok, :] = spread

    wide_rows[...] = jnp.zeros_like(wide_rows)
    for m in range(micro):
        wide = tokens[m].astype(jnp.float32)
        mean_square = jnp.mean(wide * wide, axis=1, keepdims=True)
        wide_rows[m * tok:(m + 1) * tok, :] = wide * lax.rsqrt(mean_square + 1e-06) * gain[...]
    normed[...] = wide_rows[...].astype(jnp.bfloat16)

    pl.semaphore_wait(barrier, 2 * locals_ + 1)

    def w_out(offset):
        return send(own_weights, all_weights.at[node, local], w1_send.at[offset], w1_recv.at[local],
                    (section, node, peer(offset)))

    for offset in range(1, locals_):
        w_out(offset).start()
    all_weights[node, local] = own_weights[...]

    def s1(k, offset):
        return send(normed.at[:, cut(k)], rows.at[node, local, :, cut(k)],
                    s1_send.at[k, offset], s1_recv.at[k, local], (ahead, node, peer(offset)))

    def s1_wait(k):
        for other in range(locals_):
            send(normed.at[:, cut(k)], rows.at[node, other, :, cut(k)],
                 s1_send.at[k, other], s1_recv.at[k, other], (ahead, node, local)).wait_recv()

    def s1_start(k):
        for offset in range(locals_):
            s1(k, offset).start()

    each(0, chunks, s1_start)
    carry = send(tokens, arrived, a_send, a_recv, (ahead, node, local))
    carry.start()

    def s2(k, which, block, to):
        return send(rows.at[block, :, :, cut(k)], rows.at[block, :, :, cut(k)],
                    s2_send.at[k, which], s2_recv.at[k, which], (section, to, local))

    gate_acc[...] = jnp.zeros_like(gate_acc)
    up_acc[...] = jnp.zeros_like(up_acc)

    def in_step(i):
        @pl.when(i < chunks)
        def _():
            s1_wait(i)
            s2(i, 0, node, far).start()
            s2(i, 1, node, near).start()

        @pl.when((i >= 1) & (i < chunks + 1))
        def _():
            k = i - 1
            s2(k, 0, far, far).wait_recv()
            s2(k, 2, far, near).start()

        @pl.when(i >= 2)
        def _():
            k = i - 2
            s2(k, 1, near, near).wait_recv()
            s2(k, 2, cross, near).wait_recv()
            gate_load(k).wait()
            up_load(k).wait()
            piece = rows[:, :, :, cut(k)].astype(jnp.float32).reshape(total, step).astype(jnp.bfloat16)
            gate_acc[...] += jnp.dot(piece, gate_v[cut(k), :], preferred_element_type=jnp.float32)
            up_acc[...] += jnp.dot(piece, up_v[cut(k), :], preferred_element_type=jnp.float32)

    def w2(which, block, to):
        return send(all_weights.at[block], all_weights.at[block],
                    w2_send.at[which], w2_recv.at[which], (section, to, local))

    for other in range(1, locals_):
        source = peer(other)
        send(own_weights, all_weights.at[node, source], w1_send.at[other], w1_recv.at[source],
             (section, node, source)).wait_recv()
    w2(0, node, far).start()
    w2(1, node, near).start()

    each(0, chunks + 2, in_step)

    w2(0, far, far).wait_recv()
    w2(2, far, near).start()

    gate = gate_acc[...]
    hidden = (gate / (1.0 + jnp.exp(-gate)) * up_acc[...]).astype(jnp.bfloat16)

    w2(1, near, near).wait_recv()
    w2(2, cross, near).wait_recv()
    lanes = lax.broadcasted_iota(jnp.int32, (total, LANES), 1)
    weight = jnp.sum(
        jnp.where(lanes == node, all_weights[...].reshape(total, LANES), 0.0), axis=1, keepdims=True
    )
    carry.wait_recv()
    wide_rows[...] = jnp.zeros_like(wide_rows)
    for m in range(micro):
        wide_rows[m * tok:(m + 1) * tok, :] = arrived[m].astype(jnp.float32)

    def r1(k, which, block):
        return send(parts.at[block, :, :, cut(k)], core_in.at[which, :, :, cut(k)],
                    r1_send.at[k, which], r1_recv.at[k, which], (section, near, local))

    def r2(k):
        return send(parts.at[far, :, :, cut(k)], pair_in.at[:, :, cut(k)],
                    r2_send.at[k], r2_recv.at[k], (section, far, local))

    def r3(k, offset):
        return send(sums.at[peer(offset), :, cut(k)], local_in.at[local, :, cut(k)],
                    r3_send.at[k, offset], r3_recv.at[k, local], (section, node, peer(offset)))

    def out_step(j):
        @pl.when(j < chunks)
        def _():
            down_load(j).wait()
            part = jnp.dot(hidden, down_v[:, cut(j)], preferred_element_type=jnp.float32) * weight
            parts[:, :, :, cut(j)] = part.reshape(parts.shape[:3] + (step,)).astype(jnp.bfloat16)
            r1(j, 1, cross).start()
            r1(j, 0, near).start()

        @pl.when((j >= 1) & (j < chunks + 1))
        def _():
            k = j - 1
            r1(k, 1, cross).wait_recv()
            r1(k, 0, near).wait_recv()
            both = parts[far, :, :, cut(k)].astype(jnp.float32) + core_in[1, :, :, cut(k)].astype(jnp.float32)
            parts[far, :, :, cut(k)] = both.astype(jnp.bfloat16)
            r2(k).start()

        @pl.when((j >= 2) & (j < chunks + 2))
        def _():
            k = j - 2
            r2(k).wait_recv()
            full = (
                parts[node, :, :, cut(k)].astype(jnp.float32)
                + core_in[0, :, :, cut(k)].astype(jnp.float32)
                + pair_in[:, :, cut(k)].astype(jnp.float32)
            )
            sums[:, :, cut(k)] = full.astype(jnp.bfloat16)
            for offset in range(1, locals_):
                r3(k, offset).start()

        @pl.when(j >= 3)
        def _():
            k = j - 3
            mixed = wide_rows[:, cut(k)] + sums[local, :, cut(k)].astype(jnp.float32)
            for offset in range(1, locals_):
                source = peer(offset)
                send(sums.at[source, :, cut(k)], local_in.at[source, :, cut(k)],
                     r3_send.at[k, offset], r3_recv.at[k, source], (section, node, source)).wait_recv()
                mixed += local_in[source, :, cut(k)].astype(jnp.float32)
            wide_rows[:, cut(k)] = mixed

    each(0, chunks + 3, out_step)
    for m in range(micro):
        out[m] = wide_rows[m * tok:(m + 1) * tok, :].astype(jnp.bfloat16)

    def drain(k):
        for offset in range(locals_):
            s1(k, offset).wait_send()
        s2(k, 0, node, far).wait_send()
        s2(k, 1, node, near).wait_send()
        s2(k, 2, far, near).wait_send()
        r1(k, 0, near).wait_send()
        r1(k, 1, cross).wait_send()
        r2(k).wait_send()
        for offset in range(1, locals_):
            r3(k, offset).wait_send()

    each(0, chunks, drain)
    carry.wait_send()
    for offset in range(1, locals_):
        w_out(offset).wait_send()
    w2(0, node, far).wait_send()
    w2(1, node, near).wait_send()
    w2(2, far, near).wait_send()


def shards(sections, nodes, locals_, tokens, norm_gain, routes, gate_weight, w_gate, w_up, w_down):
    width, hid = w_gate.shape[1:]
    chunks = 7
    total = nodes * locals_ * BLOCK
    bf, f32 = jnp.bfloat16, jnp.float32
    vmem, dma = pltpu.VMEM, pltpu.SemaphoreType.DMA
    here = pl.BlockSpec(memory_space=pltpu.VMEM)
    away = pl.BlockSpec(memory_space=pl.ANY)
    return pl.pallas_call(
        functools.partial(kernel, sections, locals_, chunks),
        out_shape=jax.ShapeDtypeStruct(tokens.shape, bf),
        in_specs=[here] * 4 + [away] * 3,
        out_specs=here,
        scratch_shapes=[
            vmem((width, hid), bf), vmem((width, hid), bf), vmem((hid, width), bf),
            vmem((BLOCK, width), f32), vmem((BLOCK, width), bf),
            vmem((nodes, locals_, BLOCK, width), bf),
            vmem((total, hid), f32), vmem((total, hid), f32),
            vmem(tokens.shape, bf),
            vmem((BLOCK, LANES), f32), vmem((nodes, locals_, BLOCK, LANES), f32),
            vmem((nodes, locals_, BLOCK, width), bf),
            vmem((2, locals_, BLOCK, width), bf),
            vmem((locals_, BLOCK, width), bf),
            vmem((locals_, BLOCK, width), bf),
            vmem((locals_, BLOCK, width), bf),
            dma((3, chunks)), dma, dma,
            dma((locals_,)), dma((locals_,)), dma((3,)), dma((3,)),
            dma((chunks, locals_)), dma((chunks, locals_)), dma((chunks, 3)), dma((chunks, 3)),
            dma((chunks, 2)), dma((chunks, 2)), dma((chunks,)), dma((chunks,)),
            dma((chunks, locals_)), dma((chunks, locals_)),
        ],
        compiler_params=pltpu.CompilerParams(
            collective_id=0, has_side_effects=True, vmem_limit_bytes=60 * 1024 * 1024
        ),
        cost_estimate=pl.CostEstimate(
            flops=6 * total * width * hid, bytes_accessed=6 * width * hid, transcendentals=total * hid
        ),
        name="expert_relay",
    )(tokens, norm_gain.reshape(1, width), routes, gate_weight, w_gate, w_up, w_down)


def solution(mesh):
    events = P(None, ("section", "node", "local"), None)
    sizes = (mesh.shape["section"], mesh.shape["node"], mesh.shape["local"])
    return jax.shard_map(
        functools.partial(shards, *sizes),
        mesh=mesh,
        in_specs=(events, P(), events, events, P("node", None, "local"), P("node", None, "local"), P("node", "local", None)),
        out_specs=events,
        check_vma=False,
    )
```

```python
import functools

import jax
import jax.numpy as jnp
from jax import lax
from jax.experimental import pallas as pl
from jax.experimental.pallas import tpu as pltpu
from jax.sharding import PartitionSpec as P

MESH = pl.DeviceIdType.MESH
BLOCK = 8
LANES = 128
FAR_LAG = 2
PAIR_LAG = 3


def kernel(
    sections, locals_, chunks,
    tokens, gain, routes, gate_weight, w_gate, w_up, w_down,
    out,
    gate_v, up_v, down_v, wide_rows, normed, rows, gate_acc, up_acc, arrived,
    own_weights, all_weights, parts, core_in, pair_in, sums, local_in,
    load_sem, a_send, a_recv, w1_send, w1_recv, w2_send, w2_recv,
    s1_send, s1_recv, s2_send, s2_recv, r1_send, r1_recv, r2_send, r2_recv, r3_send, r3_recv,
):
    tok, micro, width = tokens.shape
    step = width // chunks
    total = rows.shape[0] * locals_ * BLOCK
    section, node, local = (lax.axis_index(name) for name in ("section", "node", "local"))
    ahead = lax.rem(section + 1, sections)
    behind = lax.rem(section + sections - 1, sections)
    near, far, cross = node ^ 1, node ^ 2, node ^ 3

    def cut(k):
        return pl.ds(pl.multiple_of(k * step, step), step)

    def peer(offset):
        return lax.rem(local + offset, locals_)

    def each(first, last, body):
        lax.fori_loop(first, last, lambda k, c: (body(k), c)[1], 0)

    def send(src, dst, send_sem, recv_sem, to):
        return pltpu.make_async_remote_copy(
            src_ref=src, dst_ref=dst, send_sem=send_sem, recv_sem=recv_sem,
            device_id=to, device_id_type=MESH,
        )

    def gate_load(k):
        return pltpu.make_async_copy(w_gate.at[0, cut(k), :], gate_v.at[cut(k), :], load_sem.at[0, k])

    def up_load(k):
        return pltpu.make_async_copy(w_up.at[0, cut(k), :], up_v.at[cut(k), :], load_sem.at[1, k])

    def down_load(k):
        return pltpu.make_async_copy(w_down.at[0, :, cut(k)], down_v.at[:, cut(k)], load_sem.at[2, k])

    def start_in(k):
        gate_load(k).start()
        up_load(k).start()

    each(0, chunks, start_in)
    each(0, chunks, lambda k: down_load(k).start())

    barrier = pltpu.get_barrier_semaphore()
    for other in range(locals_):
        pl.semaphore_signal(barrier, inc=1, device_id=(behind, node, other), device_id_type=MESH)
    for offset in range(1, locals_):
        pl.semaphore_signal(barrier, inc=1, device_id=(section, node, peer(offset)), device_id_type=MESH)
    for other in (near, far):
        pl.semaphore_signal(barrier, inc=1, device_id=(section, other, local), device_id_type=MESH)

    own_weights[...] = jnp.zeros_like(own_weights)
    lane = lax.broadcasted_iota(jnp.int32, (routes.shape[1], LANES), 1)
    for t in range(tok):
        for m in range(micro):
            spread = jnp.where(routes[m, :, t:t + 1] == lane, gate_weight[m, :, t:t + 1], 0.0)
            own_weights[t * micro + m:t * micro + m + 1, :] = jnp.sum(spread, axis=0, keepdims=True)

    wide_rows[...] = jnp.zeros_like(wide_rows)
    for t in range(tok):
        wide = tokens[t].astype(jnp.float32)
        mean_square = jnp.mean(wide * wide, axis=1, keepdims=True)
        wide_rows[t * micro:(t + 1) * micro, :] = wide * lax.rsqrt(mean_square + 1e-06) * gain[...]
    normed[...] = wide_rows[...].astype(jnp.bfloat16)

    pl.semaphore_wait(barrier, 2 * locals_ + 1)

    def w_out(offset):
        return send(own_weights, all_weights.at[node, local], w1_send.at[offset], w1_recv.at[local],
                    (section, node, peer(offset)))

    for offset in range(1, locals_):
        w_out(offset).start()
    all_weights[node, local] = own_weights[...]

    def s1(k, offset):
        return send(normed.at[:, cut(k)], rows.at[node, local, :, cut(k)],
                    s1_send.at[k, offset], s1_recv.at[k, local], (ahead, node, peer(offset)))

    def s1_wait(k):
        for other in range(locals_):
            send(normed.at[:, cut(k)], rows.at[node, other, :, cut(k)],
                 s1_send.at[k, other], s1_recv.at[k, other], (ahead, node, local)).wait_recv()

    def s1_start(k):
        for offset in range(locals_):
            s1(k, offset).start()

    each(0, chunks, s1_start)
    carry = send(tokens, arrived, a_send, a_recv, (ahead, node, local))
    carry.start()

    def s2(k, which, block, to):
        return send(rows.at[block, :, :, cut(k)], rows.at[block, :, :, cut(k)],
                    s2_send.at[k, which], s2_recv.at[k, which], (section, to, local))

    gate_acc[...] = jnp.zeros_like(gate_acc)
    up_acc[...] = jnp.zeros_like(up_acc)

    def in_step(i):
        @pl.when(i < chunks)
        def _():
            s1_wait(i)
            s2(i, 0, node, far).start()
            s2(i, 1, node, near).start()

        @pl.when((i >= FAR_LAG) & (i < chunks + FAR_LAG))
        def _():
            k = i - FAR_LAG
            s2(k, 0, far, far).wait_recv()
            s2(k, 2, far, near).start()

        @pl.when(i > FAR_LAG)
        def _():
            k = i - FAR_LAG - 1
            s2(k, 1, near, near).wait_recv()
            s2(k, 2, cross, near).wait_recv()
            gate_load(k).wait()
            up_load(k).wait()
            piece = rows[:, :, :, cut(k)].astype(jnp.float32).reshape(total, step).astype(jnp.bfloat16)
            gate_acc[...] += jnp.dot(piece, gate_v[cut(k), :], preferred_element_type=jnp.float32)
            up_acc[...] += jnp.dot(piece, up_v[cut(k), :], preferred_element_type=jnp.float32)

    def w2(which, block, to):
        return send(all_weights.at[block], all_weights.at[block],
                    w2_send.at[which], w2_recv.at[which], (section, to, local))

    for other in range(1, locals_):
        source = peer(other)
        send(own_weights, all_weights.at[node, source], w1_send.at[other], w1_recv.at[source],
             (section, node, source)).wait_recv()
    w2(0, node, far).start()
    w2(1, node, near).start()

    each(0, chunks + FAR_LAG + 1, in_step)

    w2(0, far, far).wait_recv()
    w2(2, far, near).start()

    gate = gate_acc[...]
    hidden = (gate / (1.0 + jnp.exp(-gate)) * up_acc[...]).astype(jnp.bfloat16)

    w2(1, near, near).wait_recv()
    w2(2, cross, near).wait_recv()
    lanes = lax.broadcasted_iota(jnp.int32, (total, LANES), 1)
    weight = jnp.sum(
        jnp.where(lanes == node, all_weights[...].reshape(total, LANES), 0.0), axis=1, keepdims=True
    )
    carry.wait_recv()
    wide_rows[...] = jnp.zeros_like(wide_rows)
    for t in range(tok):
        wide_rows[t * micro:(t + 1) * micro, :] = arrived[t].astype(jnp.float32)

    def r1(k, which, block):
        return send(parts.at[block, :, :, cut(k)], core_in.at[which, :, :, cut(k)],
                    r1_send.at[k, which], r1_recv.at[k, which], (section, near, local))

    def r2(k):
        return send(parts.at[far, :, :, cut(k)], pair_in.at[:, :, cut(k)],
                    r2_send.at[k], r2_recv.at[k], (section, far, local))

    def r3(k, offset):
        return send(sums.at[peer(offset), :, cut(k)], local_in.at[local, :, cut(k)],
                    r3_send.at[k, offset], r3_recv.at[k, local], (section, node, peer(offset)))

    def out_step(j):
        @pl.when(j < chunks)
        def _():
            down_load(j).wait()
            part = jnp.dot(hidden, down_v[:, cut(j)], preferred_element_type=jnp.float32) * weight
            parts[:, :, :, cut(j)] = part.reshape(parts.shape[:3] + (step,)).astype(jnp.bfloat16)
            r1(j, 1, cross).start()
            r1(j, 0, near).start()

        @pl.when((j >= 1) & (j < chunks + 1))
        def _():
            k = j - 1
            r1(k, 1, cross).wait_recv()
            r1(k, 0, near).wait_recv()
            both = parts[far, :, :, cut(k)].astype(jnp.float32) + core_in[1, :, :, cut(k)].astype(jnp.float32)
            parts[far, :, :, cut(k)] = both.astype(jnp.bfloat16)
            r2(k).start()

        @pl.when(j >= PAIR_LAG)
        def _():
            k = j - PAIR_LAG
            r2(k).wait_recv()
            full = (
                parts[node, :, :, cut(k)].astype(jnp.float32)
                + core_in[0, :, :, cut(k)].astype(jnp.float32)
                + pair_in[:, :, cut(k)].astype(jnp.float32)
            )
            sums[:, :, cut(k)] = full.astype(jnp.bfloat16)
            for offset in range(1, locals_):
                r3(k, offset).start()

    def last_step(k):
        mixed = wide_rows[:, cut(k)] + sums[local, :, cut(k)].astype(jnp.float32)
        for offset in range(1, locals_):
            source = peer(offset)
            send(sums.at[source, :, cut(k)], local_in.at[source, :, cut(k)],
                 r3_send.at[k, offset], r3_recv.at[k, source], (section, node, source)).wait_recv()
            mixed += local_in[source, :, cut(k)].astype(jnp.float32)
        wide_rows[:, cut(k)] = mixed

    each(0, chunks + PAIR_LAG, out_step)
    each(0, chunks, last_step)
    for t in range(tok):
        out[t] = wide_rows[t * micro:(t + 1) * micro, :].astype(jnp.bfloat16)

    def drain(k):
        for offset in range(locals_):
            s1(k, offset).wait_send()
        s2(k, 0, node, far).wait_send()
        s2(k, 1, node, near).wait_send()
        s2(k, 2, far, near).wait_send()
        r1(k, 0, near).wait_send()
        r1(k, 1, cross).wait_send()
        r2(k).wait_send()
        for offset in range(1, locals_):
            r3(k, offset).wait_send()

    each(0, chunks, drain)
    carry.wait_send()
    for offset in range(1, locals_):
        w_out(offset).wait_send()
    w2(0, node, far).wait_send()
    w2(1, node, near).wait_send()
    w2(2, far, near).wait_send()


def shards(sections, nodes, locals_, tokens, norm_gain, routes, gate_weight, w_gate, w_up, w_down):
    width, hid = w_gate.shape[1:]
    chunks = 7
    total = nodes * locals_ * BLOCK
    bf, f32 = jnp.bfloat16, jnp.float32
    vmem, dma = pltpu.VMEM, pltpu.SemaphoreType.DMA
    here = pl.BlockSpec(memory_space=pltpu.VMEM)
    away = pl.BlockSpec(memory_space=pl.ANY)
    tokens = tokens.transpose(1, 0, 2)
    mixed = pl.pallas_call(
        functools.partial(kernel, sections, locals_, chunks),
        out_shape=jax.ShapeDtypeStruct(tokens.shape, bf),
        in_specs=[here] * 4 + [away] * 3,
        out_specs=here,
        scratch_shapes=[
            vmem((width, hid), bf), vmem((width, hid), bf), vmem((hid, width), bf),
            vmem((BLOCK, width), f32), vmem((BLOCK, width), bf),
            vmem((nodes, locals_, BLOCK, width), bf),
            vmem((total, hid), f32), vmem((total, hid), f32),
            vmem(tokens.shape, bf),
            vmem((BLOCK, LANES), f32), vmem((nodes, locals_, BLOCK, LANES), f32),
            vmem((nodes, locals_, BLOCK, width), bf),
            vmem((2, locals_, BLOCK, width), bf),
            vmem((locals_, BLOCK, width), bf),
            vmem((locals_, BLOCK, width), bf),
            vmem((locals_, BLOCK, width), bf),
            dma((3, chunks)), dma, dma,
            dma((locals_,)), dma((locals_,)), dma((3,)), dma((3,)),
            dma((chunks, locals_)), dma((chunks, locals_)), dma((chunks, 3)), dma((chunks, 3)),
            dma((chunks, 2)), dma((chunks, 2)), dma((chunks,)), dma((chunks,)),
            dma((chunks, locals_)), dma((chunks, locals_)),
        ],
        compiler_params=pltpu.CompilerParams(
            collective_id=0, has_side_effects=True, vmem_limit_bytes=60 * 1024 * 1024
        ),
        cost_estimate=pl.CostEstimate(
            flops=6 * total * width * hid, bytes_accessed=6 * width * hid, transcendentals=total * hid
        ),
        name="expert_relay",
    )(
        tokens, norm_gain.reshape(1, width), routes.transpose(0, 2, 1), gate_weight.transpose(0, 2, 1),
        w_gate, w_up, w_down,
    )
    return mixed.transpose(1, 0, 2)


def solution(mesh):
    events = P(None, ("section", "node", "local"), None)
    sizes = (mesh.shape["section"], mesh.shape["node"], mesh.shape["local"])
    return jax.shard_map(
        functools.partial(shards, *sizes),
        mesh=mesh,
        in_specs=(events, P(), events, events, P("node", None, "local"), P("node", None, "local"), P("node", "local", None)),
        out_specs=events,
        check_vma=False,
    )
```

```python
import functools

import jax
import jax.numpy as jnp
from jax import lax
from jax.experimental import pallas as pl
from jax.experimental.pallas import tpu as pltpu
from jax.sharding import PartitionSpec as P

MESH = pl.DeviceIdType.MESH
BLOCK = 8
LANES = 128
FAR_LAG = 2
PAIR_LAG = 3
PIECES = 4


def kernel(
    sections, locals_, chunks,
    tokens, gain, routes, gate_weight, w_gate, w_up, w_down,
    out,
    gate_v, up_v, down_v, wide_rows, packed, rows_in, rows, gate_acc, up_acc, arrived,
    own_weights, all_weights, row_weights, packing, spreading, parts, core_in, pair_in, sums, local_in,
    load_sem, a_send, a_recv, w1_send, w1_recv, w2_send, w2_recv,
    s1_send, s1_recv, s2_send, s2_recv, r1_send, r1_recv, r2_send, r2_recv, r3_send, r3_recv,
):
    tok, micro, width = tokens.shape
    step = width // chunks
    count = tok * micro
    group = locals_ * count
    total = rows.shape[0] * group
    part = step // PIECES
    pack = PIECES * count
    section, node, local = (lax.axis_index(name) for name in ("section", "node", "local"))
    ahead = lax.rem(section + 1, sections)
    behind = lax.rem(section + sections - 1, sections)
    near, far, cross = node ^ 1, node ^ 2, node ^ 3

    def cut(k):
        return pl.ds(pl.multiple_of(k * step, step), step)

    def narrow(k, p):
        return pl.ds(pl.multiple_of(k * step + p * part, part), part)

    def peer(offset):
        return lax.rem(local + offset, locals_)

    def each(first, last, body):
        lax.fori_loop(first, last, lambda k, c: (body(k), c)[1], 0)

    def send(src, dst, send_sem, recv_sem, to):
        return pltpu.make_async_remote_copy(
            src_ref=src, dst_ref=dst, send_sem=send_sem, recv_sem=recv_sem,
            device_id=to, device_id_type=MESH,
        )

    def gate_load(k):
        return pltpu.make_async_copy(w_gate.at[0, cut(k), :], gate_v.at[cut(k), :], load_sem.at[0, k])

    def up_load(k):
        return pltpu.make_async_copy(w_up.at[0, cut(k), :], up_v.at[cut(k), :], load_sem.at[1, k])

    def down_load(k):
        return pltpu.make_async_copy(w_down.at[0, :, cut(k)], down_v.at[:, cut(k)], load_sem.at[2, k])

    def start_in(k):
        gate_load(k).start()
        up_load(k).start()

    each(0, chunks, start_in)
    each(0, chunks, lambda k: down_load(k).start())

    barrier = pltpu.get_barrier_semaphore()
    for other in range(locals_):
        pl.semaphore_signal(barrier, inc=1, device_id=(behind, node, other), device_id_type=MESH)
    for offset in range(1, locals_):
        pl.semaphore_signal(barrier, inc=1, device_id=(section, node, peer(offset)), device_id_type=MESH)
    for other in (near, far):
        pl.semaphore_signal(barrier, inc=1, device_id=(section, other, local), device_id_type=MESH)

    own_weights[...] = jnp.zeros_like(own_weights)
    lane = lax.broadcasted_iota(jnp.int32, (routes.shape[1], LANES), 1)
    for t in range(tok):
        for m in range(micro):
            spread = jnp.where(routes[m, :, t:t + 1] == lane, gate_weight[m, :, t:t + 1], 0.0)
            own_weights[t * micro + m:t * micro + m + 1, :] = jnp.sum(spread, axis=0, keepdims=True)

    wide_rows[...] = jnp.zeros_like(wide_rows)
    for t in range(tok):
        wide = tokens[t].astype(jnp.float32)
        mean_square = jnp.mean(wide * wide, axis=1, keepdims=True)
        wide_rows[t * micro:(t + 1) * micro, :] = wide * lax.rsqrt(mean_square + 1e-06) * gain[...]
    packing[...] = jnp.zeros_like(packing)
    spreading[...] = jnp.zeros_like(spreading)

    def pack_own(k):
        for p in range(PIECES):
            packing[0, p * count:p * count + BLOCK, :] = wide_rows[:, narrow(k, p)]
        packed[k] = packing[0, 0:pack, :].astype(jnp.bfloat16)

    each(0, chunks, pack_own)

    pl.semaphore_wait(barrier, 2 * locals_ + 1)

    def w_out(offset):
        return send(own_weights, all_weights.at[node, local], w1_send.at[offset], w1_recv.at[local],
                    (section, node, peer(offset)))

    for offset in range(1, locals_):
        w_out(offset).start()
    all_weights[node, local] = own_weights[...]

    def s1(k, offset):
        return send(packed.at[k], rows_in.at[k, local],
                    s1_send.at[k, offset], s1_recv.at[k, local], (ahead, node, peer(offset)))

    def s1_wait(k):
        for other in range(locals_):
            send(packed.at[k], rows_in.at[k, other],
                 s1_send.at[k, other], s1_recv.at[k, other], (ahead, node, local)).wait_recv()

    def s1_start(k):
        for offset in range(locals_):
            s1(k, offset).start()

    each(0, chunks, s1_start)
    carry = send(tokens, arrived, a_send, a_recv, (ahead, node, local))
    carry.start()

    def s2(k, which, block, to):
        return send(rows.at[block, :, cut(k)], rows.at[block, :, cut(k)],
                    s2_send.at[k, which], s2_recv.at[k, which], (section, to, local))

    gate_acc[...] = jnp.zeros_like(gate_acc)
    up_acc[...] = jnp.zeros_like(up_acc)

    def in_step(i):
        @pl.when(i < chunks)
        def _():
            s1_wait(i)
            for other in range(locals_):
                packing[other, 0:pack, :] = rows_in[i, other].astype(jnp.float32)
                for p in range(PIECES):
                    spreading[other * count:other * count + BLOCK, p * part:(p + 1) * part] = (
                        packing[other, p * count:p * count + BLOCK, :]
                    )
            rows[node, :, cut(i)] = spreading[0:group, :].astype(jnp.bfloat16)
            s2(i, 0, node, far).start()
            s2(i, 1, node, near).start()

        @pl.when((i >= FAR_LAG) & (i < chunks + FAR_LAG))
        def _():
            k = i - FAR_LAG
            s2(k, 0, far, far).wait_recv()
            s2(k, 2, far, near).start()

        @pl.when(i > FAR_LAG)
        def _():
            k = i - FAR_LAG - 1
            s2(k, 1, near, near).wait_recv()
            s2(k, 2, cross, near).wait_recv()
            gate_load(k).wait()
            up_load(k).wait()
            piece = rows[:, :, cut(k)].astype(jnp.float32).reshape(total, step).astype(jnp.bfloat16)
            gate_acc[...] += jnp.dot(piece, gate_v[cut(k), :], preferred_element_type=jnp.float32)
            up_acc[...] += jnp.dot(piece, up_v[cut(k), :], preferred_element_type=jnp.float32)

    def w2(which, block, to):
        return send(all_weights.at[block], all_weights.at[block],
                    w2_send.at[which], w2_recv.at[which], (section, to, local))

    for other in range(1, locals_):
        source = peer(other)
        send(own_weights, all_weights.at[node, source], w1_send.at[other], w1_recv.at[source],
             (section, node, source)).wait_recv()
    w2(0, node, far).start()
    w2(1, node, near).start()

    each(0, chunks + FAR_LAG + 1, in_step)

    w2(0, far, far).wait_recv()
    w2(2, far, near).start()

    gate = gate_acc[...]
    hidden = (gate / (1.0 + jnp.exp(-gate)) * up_acc[...]).astype(jnp.bfloat16)

    w2(1, near, near).wait_recv()
    w2(2, cross, near).wait_recv()
    for block in range(rows.shape[0]):
        for other in range(locals_):
            first = block * group + other * count
            row_weights[first:first + BLOCK, :] = all_weights[block, other]
    lanes = lax.broadcasted_iota(jnp.int32, (total, LANES), 1)
    weight = jnp.sum(jnp.where(lanes == node, row_weights[0:total, :], 0.0), axis=1, keepdims=True)
    carry.wait_recv()
    wide_rows[...] = jnp.zeros_like(wide_rows)
    for t in range(tok):
        wide_rows[t * micro:(t + 1) * micro, :] = arrived[t].astype(jnp.float32)

    def r1(k, which, block):
        return send(parts.at[block, :, cut(k)], core_in.at[which, :, cut(k)],
                    r1_send.at[k, which], r1_recv.at[k, which], (section, near, local))

    def r2(k):
        return send(parts.at[far, :, cut(k)], pair_in.at[:, cut(k)],
                    r2_send.at[k], r2_recv.at[k], (section, far, local))

    def r3(k, offset):
        return send(sums.at[k, peer(offset)], local_in.at[k, local],
                    r3_send.at[k, offset], r3_recv.at[k, local], (section, node, peer(offset)))

    def out_step(j):
        @pl.when(j < chunks)
        def _():
            down_load(j).wait()
            term = jnp.dot(hidden, down_v[:, cut(j)], preferred_element_type=jnp.float32) * weight
            parts[:, :, cut(j)] = term.reshape(parts.shape[:2] + (step,)).astype(jnp.bfloat16)
            r1(j, 1, cross).start()
            r1(j, 0, near).start()

        @pl.when((j >= 1) & (j < chunks + 1))
        def _():
            k = j - 1
            r1(k, 1, cross).wait_recv()
            r1(k, 0, near).wait_recv()
            both = parts[far, :, cut(k)].astype(jnp.float32) + core_in[1, :, cut(k)].astype(jnp.float32)
            parts[far, :, cut(k)] = both.astype(jnp.bfloat16)
            r2(k).start()

        @pl.when(j >= PAIR_LAG)
        def _():
            k = j - PAIR_LAG
            r2(k).wait_recv()
            spreading[0:group, :] = (
                parts[node, :, cut(k)].astype(jnp.float32)
                + core_in[0, :, cut(k)].astype(jnp.float32)
                + pair_in[:, cut(k)].astype(jnp.float32)
            )
            for other in range(locals_):
                for p in range(PIECES):
                    packing[other, p * count:p * count + BLOCK, :] = (
                        spreading[other * count:other * count + BLOCK, p * part:(p + 1) * part]
                    )
                sums[k, other] = packing[other, 0:pack, :].astype(jnp.bfloat16)
            for offset in range(1, locals_):
                r3(k, offset).start()

    def last_step(k):
        mixed = sums[k, local].astype(jnp.float32)
        for offset in range(1, locals_):
            source = peer(offset)
            send(sums.at[k, source], local_in.at[k, source],
                 r3_send.at[k, offset], r3_recv.at[k, source], (section, node, source)).wait_recv()
            mixed += local_in[k, source].astype(jnp.float32)
        packing[0, 0:pack, :] = mixed
        for p in range(PIECES):
            wide_rows[:, narrow(k, p)] += packing[0, p * count:p * count + BLOCK, :]

    each(0, chunks + PAIR_LAG, out_step)
    each(0, chunks, last_step)
    for t in range(tok):
        out[t] = wide_rows[t * micro:(t + 1) * micro, :].astype(jnp.bfloat16)

    def drain(k):
        for offset in range(locals_):
            s1(k, offset).wait_send()
        s2(k, 0, node, far).wait_send()
        s2(k, 1, node, near).wait_send()
        s2(k, 2, far, near).wait_send()
        r1(k, 0, near).wait_send()
        r1(k, 1, cross).wait_send()
        r2(k).wait_send()
        for offset in range(1, locals_):
            r3(k, offset).wait_send()

    each(0, chunks, drain)
    carry.wait_send()
    for offset in range(1, locals_):
        w_out(offset).wait_send()
    w2(0, node, far).wait_send()
    w2(1, node, near).wait_send()
    w2(2, far, near).wait_send()


def shards(sections, nodes, locals_, tokens, norm_gain, routes, gate_weight, w_gate, w_up, w_down):
    width, hid = w_gate.shape[1:]
    chunks = 7
    count = tokens.shape[0] * tokens.shape[1]
    group = locals_ * count
    total = nodes * group
    step = width // chunks
    pack, part = PIECES * count, step // PIECES
    bf, f32 = jnp.bfloat16, jnp.float32
    vmem, dma = pltpu.VMEM, pltpu.SemaphoreType.DMA
    here = pl.BlockSpec(memory_space=pltpu.VMEM)
    away = pl.BlockSpec(memory_space=pl.ANY)
    tokens = tokens.transpose(1, 0, 2)
    mixed = pl.pallas_call(
        functools.partial(kernel, sections, locals_, chunks),
        out_shape=jax.ShapeDtypeStruct(tokens.shape, bf),
        in_specs=[here] * 4 + [away] * 3,
        out_specs=here,
        scratch_shapes=[
            vmem((width, hid), bf), vmem((width, hid), bf), vmem((hid, width), bf),
            vmem((BLOCK, width), f32), vmem((chunks, pack, part), bf),
            vmem((chunks, locals_, pack, part), bf),
            vmem((nodes, group, width), bf),
            vmem((total, hid), f32), vmem((total, hid), f32),
            vmem(tokens.shape, bf),
            vmem((BLOCK, LANES), f32), vmem((nodes, locals_, BLOCK, LANES), f32),
            vmem((total + BLOCK, LANES), f32),
            vmem((locals_, pack + BLOCK, part), f32), vmem((group + BLOCK, step), f32),
            vmem((nodes, group, width), bf),
            vmem((2, group, width), bf),
            vmem((group, width), bf),
            vmem((chunks, locals_, pack, part), bf),
            vmem((chunks, locals_, pack, part), bf),
            dma((3, chunks)), dma, dma,
            dma((locals_,)), dma((locals_,)), dma((3,)), dma((3,)),
            dma((chunks, locals_)), dma((chunks, locals_)), dma((chunks, 3)), dma((chunks, 3)),
            dma((chunks, 2)), dma((chunks, 2)), dma((chunks,)), dma((chunks,)),
            dma((chunks, locals_)), dma((chunks, locals_)),
        ],
        compiler_params=pltpu.CompilerParams(
            collective_id=0, has_side_effects=True, vmem_limit_bytes=60 * 1024 * 1024
        ),
        cost_estimate=pl.CostEstimate(
            flops=6 * total * width * hid, bytes_accessed=6 * width * hid, transcendentals=total * hid
        ),
        name="expert_relay",
    )(
        tokens, norm_gain.reshape(1, width), routes.transpose(0, 2, 1), gate_weight.transpose(0, 2, 1),
        w_gate, w_up, w_down,
    )
    return mixed.transpose(1, 0, 2)


def solution(mesh):
    events = P(None, ("section", "node", "local"), None)
    sizes = (mesh.shape["section"], mesh.shape["node"], mesh.shape["local"])
    return jax.shard_map(
        functools.partial(shards, *sizes),
        mesh=mesh,
        in_specs=(events, P(), events, events, P("node", None, "local"), P("node", None, "local"), P("node", "local", None)),
        out_specs=events,
        check_vma=False,
    )
```

```python
import functools

import jax
import jax.numpy as jnp
from jax import lax
from jax.experimental import pallas as pl
from jax.experimental.pallas import tpu as pltpu
from jax.sharding import PartitionSpec as P

MESH = pl.DeviceIdType.MESH
BLOCK = 8
LANES = 128
FAR_LAG = 2
CORE_LAG = 2
PAIR_LAG = 4
PIECES = 4


def kernel(
    sections, locals_, chunks,
    tokens, gain, routes, gate_weight, w_gate, w_up, w_down,
    out,
    gate_v, up_v, down_v, wide_rows, packed, rows_in, rows, gate_acc, up_acc, arrived,
    own_weights, all_weights, row_weights, packing, spreading, parts, core_in, pair_in, sums, local_in,
    load_sem, a_send, a_recv, w1_send, w1_recv, w2_send, w2_recv,
    s1_send, s1_recv, s2_send, s2_recv, r1_send, r1_recv, r2_send, r2_recv, r3_send, r3_recv,
):
    tok, micro, width = tokens.shape
    step = width // chunks
    count = tok * micro
    group = locals_ * count
    total = rows.shape[0] * group
    part = step // PIECES
    pack = PIECES * count
    section, node, local = (lax.axis_index(name) for name in ("section", "node", "local"))
    ahead = lax.rem(section + 1, sections)
    behind = lax.rem(section + sections - 1, sections)
    near, far, cross = node ^ 1, node ^ 2, node ^ 3

    def cut(k):
        return pl.ds(pl.multiple_of(k * step, step), step)

    def narrow(k, p):
        return pl.ds(pl.multiple_of(k * step + p * part, part), part)

    def peer(offset):
        return lax.rem(local + offset, locals_)

    def each(first, last, body):
        lax.fori_loop(first, last, lambda k, c: (body(k), c)[1], 0)

    def send(src, dst, send_sem, recv_sem, to):
        return pltpu.make_async_remote_copy(
            src_ref=src, dst_ref=dst, send_sem=send_sem, recv_sem=recv_sem,
            device_id=to, device_id_type=MESH,
        )

    def gate_load(k):
        return pltpu.make_async_copy(w_gate.at[0, cut(k), :], gate_v.at[cut(k), :], load_sem.at[0, k])

    def up_load(k):
        return pltpu.make_async_copy(w_up.at[0, cut(k), :], up_v.at[cut(k), :], load_sem.at[1, k])

    def down_load(k):
        return pltpu.make_async_copy(w_down.at[0, :, cut(k)], down_v.at[:, cut(k)], load_sem.at[2, k])

    def start_in(k):
        gate_load(k).start()
        up_load(k).start()

    barrier = pltpu.get_barrier_semaphore()
    for other in range(locals_):
        pl.semaphore_signal(barrier, inc=1, device_id=(behind, node, other), device_id_type=MESH)
    for offset in range(1, locals_):
        pl.semaphore_signal(barrier, inc=1, device_id=(section, node, peer(offset)), device_id_type=MESH)
    for other in (near, far):
        pl.semaphore_signal(barrier, inc=1, device_id=(section, other, local), device_id_type=MESH)

    each(0, chunks, start_in)
    each(0, chunks, lambda k: down_load(k).start())

    own_weights[...] = jnp.zeros_like(own_weights)
    lane = lax.broadcasted_iota(jnp.int32, (routes.shape[1], LANES), 1)
    for t in range(tok):
        for m in range(micro):
            spread = jnp.where(routes[m, :, t:t + 1] == lane, gate_weight[m, :, t:t + 1], 0.0)
            own_weights[t * micro + m:t * micro + m + 1, :] = jnp.sum(spread, axis=0, keepdims=True)

    wide_rows[...] = jnp.zeros_like(wide_rows)
    for t in range(tok):
        wide = tokens[t].astype(jnp.float32)
        mean_square = jnp.mean(wide * wide, axis=1, keepdims=True)
        wide_rows[t * micro:(t + 1) * micro, :] = wide * lax.rsqrt(mean_square + 1e-06) * gain[...]
    packing[...] = jnp.zeros_like(packing)
    spreading[...] = jnp.zeros_like(spreading)

    def pack_own(k):
        for p in range(PIECES):
            packing[0, p * count:p * count + BLOCK, :] = wide_rows[:, narrow(k, p)]
        packed[k] = packing[0, 0:pack, :].astype(jnp.bfloat16)

    each(0, chunks, pack_own)

    pl.semaphore_wait(barrier, 2 * locals_ + 1)

    def w_out(offset):
        return send(own_weights, all_weights.at[node, local], w1_send.at[offset], w1_recv.at[local],
                    (section, node, peer(offset)))

    for offset in range(1, locals_):
        w_out(offset).start()
    all_weights[node, local] = own_weights[...]

    def s1(k, offset):
        return send(packed.at[k], rows_in.at[k, local],
                    s1_send.at[k, offset], s1_recv.at[k, local], (ahead, node, peer(offset)))

    def s1_wait(k):
        for other in range(locals_):
            send(packed.at[k], rows_in.at[k, other],
                 s1_send.at[k, other], s1_recv.at[k, other], (ahead, node, local)).wait_recv()

    def s1_start(k):
        for offset in range(locals_):
            s1(k, offset).start()

    each(0, chunks, s1_start)
    carry = send(tokens, arrived, a_send, a_recv, (ahead, node, local))
    carry.start()

    def s2(k, which, block, to):
        return send(rows.at[block, :, cut(k)], rows.at[block, :, cut(k)],
                    s2_send.at[k, which], s2_recv.at[k, which], (section, to, local))

    gate_acc[...] = jnp.zeros_like(gate_acc)
    up_acc[...] = jnp.zeros_like(up_acc)

    def w2(which, block, to):
        return send(all_weights.at[block], all_weights.at[block],
                    w2_send.at[which], w2_recv.at[which], (section, to, local))

    def in_step(i):
        @pl.when(i < chunks)
        def _():
            s1_wait(i)
            for other in range(locals_):
                packing[other, 0:pack, :] = rows_in[i, other].astype(jnp.float32)
                for p in range(PIECES):
                    spreading[other * count:other * count + BLOCK, p * part:(p + 1) * part] = (
                        packing[other, p * count:p * count + BLOCK, :]
                    )
            rows[node, :, cut(i)] = spreading[0:group, :].astype(jnp.bfloat16)
            s2(i, 0, node, far).start()
            s2(i, 1, node, near).start()

        @pl.when(i == 1)
        def _():
            for other in range(1, locals_):
                source = peer(other)
                send(own_weights, all_weights.at[node, source], w1_send.at[other], w1_recv.at[source],
                     (section, node, source)).wait_recv()
            w2(0, node, far).start()
            w2(1, node, near).start()

        @pl.when(i == chunks)
        def _():
            w2(0, far, far).wait_recv()
            w2(2, far, near).start()

        @pl.when((i >= FAR_LAG) & (i < chunks + FAR_LAG))
        def _():
            k = i - FAR_LAG
            s2(k, 0, far, far).wait_recv()
            s2(k, 2, far, near).start()

        @pl.when(i > FAR_LAG)
        def _():
            k = i - FAR_LAG - 1
            s2(k, 1, near, near).wait_recv()
            s2(k, 2, cross, near).wait_recv()
            gate_load(k).wait()
            up_load(k).wait()
            piece = rows[:, :, cut(k)].astype(jnp.float32).reshape(total, step).astype(jnp.bfloat16)
            gate_acc[...] += jnp.dot(piece, gate_v[cut(k), :], preferred_element_type=jnp.float32)
            up_acc[...] += jnp.dot(piece, up_v[cut(k), :], preferred_element_type=jnp.float32)

    each(0, chunks + FAR_LAG + 1, in_step)

    gate = gate_acc[...]
    hidden = (gate / (1.0 + jnp.exp(-gate)) * up_acc[...]).astype(jnp.bfloat16)

    w2(1, near, near).wait_recv()
    w2(2, cross, near).wait_recv()
    for block in range(rows.shape[0]):
        for other in range(locals_):
            first = block * group + other * count
            row_weights[first:first + BLOCK, :] = all_weights[block, other]
    lanes = lax.broadcasted_iota(jnp.int32, (total, LANES), 1)
    weight = jnp.sum(jnp.where(lanes == node, row_weights[0:total, :], 0.0), axis=1, keepdims=True)

    def r1(k, which, block):
        return send(parts.at[block, :, cut(k)], core_in.at[which, :, cut(k)],
                    r1_send.at[k, which], r1_recv.at[k, which], (section, near, local))

    def r2(k):
        return send(parts.at[far, :, cut(k)], pair_in.at[:, cut(k)],
                    r2_send.at[k], r2_recv.at[k], (section, far, local))

    def r3(k, offset):
        return send(sums.at[k, peer(offset)], local_in.at[k, local],
                    r3_send.at[k, offset], r3_recv.at[k, local], (section, node, peer(offset)))

    def out_step(j):
        @pl.when(j == chunks)
        def _():
            carry.wait_recv()
            wide_rows[...] = jnp.zeros_like(wide_rows)
            for t in range(tok):
                wide_rows[t * micro:(t + 1) * micro, :] = arrived[t].astype(jnp.float32)

        @pl.when(j < chunks)
        def _():
            down_load(j).wait()
            term = jnp.dot(hidden, down_v[:, cut(j)], preferred_element_type=jnp.float32) * weight
            parts[:, :, cut(j)] = term.reshape(parts.shape[:2] + (step,)).astype(jnp.bfloat16)
            r1(j, 1, cross).start()
            r1(j, 0, near).start()
            for offset in range(locals_):
                s1(j, offset).wait_send()
            s2(j, 0, node, far).wait_send()
            s2(j, 1, node, near).wait_send()
            s2(j, 2, far, near).wait_send()

        @pl.when((j >= CORE_LAG) & (j < chunks + CORE_LAG))
        def _():
            k = j - CORE_LAG
            r1(k, 1, cross).wait_recv()
            r1(k, 0, near).wait_recv()
            both = parts[far, :, cut(k)].astype(jnp.float32) + core_in[1, :, cut(k)].astype(jnp.float32)
            parts[far, :, cut(k)] = both.astype(jnp.bfloat16)
            r2(k).start()

        @pl.when(j >= PAIR_LAG)
        def _():
            k = j - PAIR_LAG
            r2(k).wait_recv()
            spreading[0:group, :] = (
                parts[node, :, cut(k)].astype(jnp.float32)
                + core_in[0, :, cut(k)].astype(jnp.float32)
                + pair_in[:, cut(k)].astype(jnp.float32)
            )
            for other in range(locals_):
                for p in range(PIECES):
                    packing[other, p * count:p * count + BLOCK, :] = (
                        spreading[other * count:other * count + BLOCK, p * part:(p + 1) * part]
                    )
                sums[k, other] = packing[other, 0:pack, :].astype(jnp.bfloat16)
            for offset in range(1, locals_):
                r3(k, offset).start()

    def last_step(k):
        r1(k, 0, near).wait_send()
        r1(k, 1, cross).wait_send()
        r2(k).wait_send()
        for offset in range(1, locals_):
            r3(k, offset).wait_send()
        mixed = sums[k, local].astype(jnp.float32)
        for offset in range(1, locals_):
            source = peer(offset)
            send(sums.at[k, source], local_in.at[k, source],
                 r3_send.at[k, offset], r3_recv.at[k, source], (section, node, source)).wait_recv()
            mixed += local_in[k, source].astype(jnp.float32)
        packing[0, 0:pack, :] = mixed
        for p in range(PIECES):
            wide_rows[:, narrow(k, p)] += packing[0, p * count:p * count + BLOCK, :]

    each(0, chunks + PAIR_LAG, out_step)
    carry.wait_send()
    for offset in range(1, locals_):
        w_out(offset).wait_send()
    w2(0, node, far).wait_send()
    w2(1, node, near).wait_send()
    w2(2, far, near).wait_send()

    each(0, chunks, last_step)
    for t in range(tok):
        out[t] = wide_rows[t * micro:(t + 1) * micro, :].astype(jnp.bfloat16)


def shards(sections, nodes, locals_, tokens, norm_gain, routes, gate_weight, w_gate, w_up, w_down):
    width, hid = w_gate.shape[1:]
    chunks = 7
    count = tokens.shape[0] * tokens.shape[1]
    group = locals_ * count
    total = nodes * group
    step = width // chunks
    pack, part = PIECES * count, step // PIECES
    bf, f32 = jnp.bfloat16, jnp.float32
    vmem, dma = pltpu.VMEM, pltpu.SemaphoreType.DMA
    here = pl.BlockSpec(memory_space=pltpu.VMEM)
    away = pl.BlockSpec(memory_space=pl.ANY)
    tokens = tokens.transpose(1, 0, 2)
    mixed = pl.pallas_call(
        functools.partial(kernel, sections, locals_, chunks),
        out_shape=jax.ShapeDtypeStruct(tokens.shape, bf),
        in_specs=[here] * 4 + [away] * 3,
        out_specs=here,
        scratch_shapes=[
            vmem((width, hid), bf), vmem((width, hid), bf), vmem((hid, width), bf),
            vmem((BLOCK, width), f32), vmem((chunks, pack, part), bf),
            vmem((chunks, locals_, pack, part), bf),
            vmem((nodes, group, width), bf),
            vmem((total, hid), f32), vmem((total, hid), f32),
            vmem(tokens.shape, bf),
            vmem((BLOCK, LANES), f32), vmem((nodes, locals_, BLOCK, LANES), f32),
            vmem((total + BLOCK, LANES), f32),
            vmem((locals_, pack + BLOCK, part), f32), vmem((group + BLOCK, step), f32),
            vmem((nodes, group, width), bf),
            vmem((2, group, width), bf),
            vmem((group, width), bf),
            vmem((chunks, locals_, pack, part), bf),
            vmem((chunks, locals_, pack, part), bf),
            dma((3, chunks)), dma, dma,
            dma((locals_,)), dma((locals_,)), dma((3,)), dma((3,)),
            dma((chunks, locals_)), dma((chunks, locals_)), dma((chunks, 3)), dma((chunks, 3)),
            dma((chunks, 2)), dma((chunks, 2)), dma((chunks,)), dma((chunks,)),
            dma((chunks, locals_)), dma((chunks, locals_)),
        ],
        compiler_params=pltpu.CompilerParams(
            collective_id=0, has_side_effects=True, vmem_limit_bytes=60 * 1024 * 1024
        ),
        cost_estimate=pl.CostEstimate(
            flops=6 * total * width * hid, bytes_accessed=6 * width * hid, transcendentals=total * hid
        ),
        name="expert_relay",
    )(
        tokens, norm_gain.reshape(1, width), routes.transpose(0, 2, 1), gate_weight.transpose(0, 2, 1),
        w_gate, w_up, w_down,
    )
    return mixed.transpose(1, 0, 2)


def solution(mesh):
    events = P(None, ("section", "node", "local"), None)
    sizes = (mesh.shape["section"], mesh.shape["node"], mesh.shape["local"])
    return jax.shard_map(
        functools.partial(shards, *sizes),
        mesh=mesh,
        in_specs=(events, P(), events, events, P("node", None, "local"), P("node", None, "local"), P("node", "local", None)),
        out_specs=events,
        check_vma=False,
    )
```

```python
import functools

import jax
import jax.numpy as jnp
from jax import lax
from jax.experimental import pallas as pl
from jax.experimental.pallas import tpu as pltpu
from jax.sharding import PartitionSpec as P

MESH = pl.DeviceIdType.MESH
BLOCK = 8
LANES = 128
FAR_LAG = 2
CORE_LAG = 2
PAIR_LAG = 4
PIECES = 4


def kernel(
    sections, locals_, chunks,
    tokens, gain, routes, gate_weight, w_gate, w_up, w_down,
    out,
    both_v, down_v, wide_rows, packed, rows_in, rows, acts, arrived,
    own_weights, all_weights, row_weights, packing, spreading, parts, core_in, pair_in, sums, local_in,
    load_sem, a_send, a_recv, w1_send, w1_recv, w2_send, w2_recv,
    s1_send, s1_recv, s2_send, s2_recv, r1_send, r1_recv, r2_send, r2_recv, r3_send, r3_recv,
):
    tok, micro, width = tokens.shape
    hid = down_v.shape[0]
    step = width // chunks
    count = tok * micro
    group = locals_ * count
    total = rows.shape[0] * group
    part = step // PIECES
    pack = PIECES * count
    section, node, local = (lax.axis_index(name) for name in ("section", "node", "local"))
    ahead = lax.rem(section + 1, sections)
    behind = lax.rem(section + sections - 1, sections)
    near, far, cross = node ^ 1, node ^ 2, node ^ 3

    def cut(k):
        return pl.ds(pl.multiple_of(k * step, step), step)

    def narrow(k, p):
        return pl.ds(pl.multiple_of(k * step + p * part, part), part)

    def peer(offset):
        return lax.rem(local + offset, locals_)

    def each(first, last, body):
        lax.fori_loop(first, last, lambda k, c: (body(k), c)[1], 0)

    def send(src, dst, send_sem, recv_sem, to):
        return pltpu.make_async_remote_copy(
            src_ref=src, dst_ref=dst, send_sem=send_sem, recv_sem=recv_sem,
            device_id=to, device_id_type=MESH,
        )

    def gate_load(k):
        return pltpu.make_async_copy(w_gate.at[0, cut(k), :], both_v.at[cut(k), 0:hid], load_sem.at[0, k])

    def up_load(k):
        return pltpu.make_async_copy(w_up.at[0, cut(k), :], both_v.at[cut(k), hid:2 * hid], load_sem.at[1, k])

    def down_load(k):
        return pltpu.make_async_copy(w_down.at[0, :, cut(k)], down_v.at[:, cut(k)], load_sem.at[2, k])

    def start_in(k):
        gate_load(k).start()
        up_load(k).start()

    barrier = pltpu.get_barrier_semaphore()
    for other in range(locals_):
        pl.semaphore_signal(barrier, inc=1, device_id=(behind, node, other), device_id_type=MESH)
    for offset in range(1, locals_):
        pl.semaphore_signal(barrier, inc=1, device_id=(section, node, peer(offset)), device_id_type=MESH)
    for other in (near, far):
        pl.semaphore_signal(barrier, inc=1, device_id=(section, other, local), device_id_type=MESH)

    each(0, chunks, start_in)
    each(0, chunks, lambda k: down_load(k).start())

    own_weights[...] = jnp.zeros_like(own_weights)
    lane = lax.broadcasted_iota(jnp.int32, (routes.shape[1], LANES), 1)
    for t in range(tok):
        for m in range(micro):
            spread = jnp.where(routes[m, :, t:t + 1] == lane, gate_weight[m, :, t:t + 1], 0.0)
            own_weights[t * micro + m:t * micro + m + 1, :] = jnp.sum(spread, axis=0, keepdims=True)

    wide_rows[...] = jnp.zeros_like(wide_rows)
    for t in range(tok):
        wide = tokens[t].astype(jnp.float32)
        mean_square = jnp.mean(wide * wide, axis=1, keepdims=True)
        wide_rows[t * micro:(t + 1) * micro, :] = wide * lax.rsqrt(mean_square + 1e-06) * gain[...]
    packing[...] = jnp.zeros_like(packing)
    spreading[...] = jnp.zeros_like(spreading)

    def pack_own(k):
        for p in range(PIECES):
            packing[0, p * count:p * count + BLOCK, :] = wide_rows[:, narrow(k, p)]
        packed[k] = packing[0, 0:pack, :].astype(jnp.bfloat16)


    pl.semaphore_wait(barrier, 2 * locals_ + 1)

    def w_out(offset):
        return send(own_weights, all_weights.at[node, local], w1_send.at[offset], w1_recv.at[local],
                    (section, node, peer(offset)))

    for offset in range(1, locals_):
        w_out(offset).start()
    all_weights[node, local] = own_weights[...]

    def s1(k, offset):
        return send(packed.at[k], rows_in.at[k, local],
                    s1_send.at[k, offset], s1_recv.at[k, local], (ahead, node, peer(offset)))

    def s1_wait(k):
        for other in range(locals_):
            send(packed.at[k], rows_in.at[k, other],
                 s1_send.at[k, other], s1_recv.at[k, other], (ahead, node, local)).wait_recv()

    def s1_start(k):
        pack_own(k)
        for offset in range(locals_):
            s1(k, offset).start()

    each(0, chunks, s1_start)
    carry = send(tokens, arrived, a_send, a_recv, (ahead, node, local))
    carry.start()

    def s2(k, which, block, to):
        return send(rows.at[block, :, cut(k)], rows.at[block, :, cut(k)],
                    s2_send.at[k, which], s2_recv.at[k, which], (section, to, local))

    acts[...] = jnp.zeros_like(acts)

    def w2(which, block, to):
        return send(all_weights.at[block], all_weights.at[block],
                    w2_send.at[which], w2_recv.at[which], (section, to, local))

    def in_step(i):
        @pl.when(i < chunks)
        def _():
            s1_wait(i)
            for other in range(locals_):
                packing[other, 0:pack, :] = rows_in[i, other].astype(jnp.float32)
                for p in range(PIECES):
                    spreading[other * count:other * count + BLOCK, p * part:(p + 1) * part] = (
                        packing[other, p * count:p * count + BLOCK, :]
                    )
            rows[node, :, cut(i)] = spreading[0:group, :].astype(jnp.bfloat16)
            s2(i, 0, node, far).start()
            s2(i, 1, node, near).start()

        @pl.when(i == 1)
        def _():
            for other in range(1, locals_):
                source = peer(other)
                send(own_weights, all_weights.at[node, source], w1_send.at[other], w1_recv.at[source],
                     (section, node, source)).wait_recv()
            w2(0, node, far).start()
            w2(1, node, near).start()

        @pl.when(i == chunks)
        def _():
            w2(0, far, far).wait_recv()
            w2(2, far, near).start()

        @pl.when((i >= FAR_LAG) & (i < chunks + FAR_LAG))
        def _():
            k = i - FAR_LAG
            s2(k, 0, far, far).wait_recv()
            s2(k, 2, far, near).start()

        @pl.when(i > FAR_LAG)
        def _():
            k = i - FAR_LAG - 1
            s2(k, 1, near, near).wait_recv()
            s2(k, 2, cross, near).wait_recv()
            gate_load(k).wait()
            up_load(k).wait()
            piece = rows[:, :, cut(k)].astype(jnp.float32).reshape(total, step).astype(jnp.bfloat16)
            acts[...] += jnp.dot(piece, both_v[cut(k), :], preferred_element_type=jnp.float32)

    each(0, chunks + FAR_LAG + 1, in_step)

    gate = acts[:, 0:hid]
    hidden = (gate / (1.0 + jnp.exp(-gate)) * acts[:, hid:2 * hid]).astype(jnp.bfloat16)

    w2(1, near, near).wait_recv()
    w2(2, cross, near).wait_recv()
    for block in range(rows.shape[0]):
        for other in range(locals_):
            first = block * group + other * count
            row_weights[first:first + BLOCK, :] = all_weights[block, other]
    lanes = lax.broadcasted_iota(jnp.int32, (total, LANES), 1)
    weight = jnp.sum(jnp.where(lanes == node, row_weights[0:total, :], 0.0), axis=1, keepdims=True)

    def r1(k, which, block):
        return send(parts.at[block, :, cut(k)], core_in.at[which, :, cut(k)],
                    r1_send.at[k, which], r1_recv.at[k, which], (section, near, local))

    def r2(k):
        return send(parts.at[far, :, cut(k)], pair_in.at[:, cut(k)],
                    r2_send.at[k], r2_recv.at[k], (section, far, local))

    def r3(k, offset):
        return send(sums.at[k, peer(offset)], local_in.at[k, local],
                    r3_send.at[k, offset], r3_recv.at[k, local], (section, node, peer(offset)))

    def out_step(j):
        @pl.when(j == chunks)
        def _():
            carry.wait_recv()
            wide_rows[...] = jnp.zeros_like(wide_rows)
            for t in range(tok):
                wide_rows[t * micro:(t + 1) * micro, :] = arrived[t].astype(jnp.float32)

        @pl.when(j < chunks)
        def _():
            down_load(j).wait()
            term = jnp.dot(hidden, down_v[:, cut(j)], preferred_element_type=jnp.float32) * weight
            parts[:, :, cut(j)] = term.reshape(parts.shape[:2] + (step,)).astype(jnp.bfloat16)
            r1(j, 1, cross).start()
            r1(j, 0, near).start()
            for offset in range(locals_):
                s1(j, offset).wait_send()
            s2(j, 0, node, far).wait_send()
            s2(j, 1, node, near).wait_send()
            s2(j, 2, far, near).wait_send()

        @pl.when((j >= CORE_LAG) & (j < chunks + CORE_LAG))
        def _():
            k = j - CORE_LAG
            r1(k, 1, cross).wait_recv()
            r1(k, 0, near).wait_recv()
            both = parts[far, :, cut(k)].astype(jnp.float32) + core_in[1, :, cut(k)].astype(jnp.float32)
            parts[far, :, cut(k)] = both.astype(jnp.bfloat16)
            r2(k).start()

        @pl.when(j >= PAIR_LAG)
        def _():
            k = j - PAIR_LAG
            r2(k).wait_recv()
            spreading[0:group, :] = (
                parts[node, :, cut(k)].astype(jnp.float32)
                + core_in[0, :, cut(k)].astype(jnp.float32)
                + pair_in[:, cut(k)].astype(jnp.float32)
            )
            for other in range(locals_):
                for p in range(PIECES):
                    packing[other, p * count:p * count + BLOCK, :] = (
                        spreading[other * count:other * count + BLOCK, p * part:(p + 1) * part]
                    )
                sums[k, other] = packing[other, 0:pack, :].astype(jnp.bfloat16)
            for offset in range(1, locals_):
                r3(k, offset).start()

    def last_step(k):
        r1(k, 0, near).wait_send()
        r1(k, 1, cross).wait_send()
        r2(k).wait_send()
        for offset in range(1, locals_):
            r3(k, offset).wait_send()
        mixed = sums[k, local].astype(jnp.float32)
        for offset in range(1, locals_):
            source = peer(offset)
            send(sums.at[k, source], local_in.at[k, source],
                 r3_send.at[k, offset], r3_recv.at[k, source], (section, node, source)).wait_recv()
            mixed += local_in[k, source].astype(jnp.float32)
        packing[0, 0:pack, :] = mixed
        for p in range(PIECES):
            wide_rows[:, narrow(k, p)] += packing[0, p * count:p * count + BLOCK, :]

    each(0, chunks + PAIR_LAG, out_step)
    carry.wait_send()
    for offset in range(1, locals_):
        w_out(offset).wait_send()
    w2(0, node, far).wait_send()
    w2(1, node, near).wait_send()
    w2(2, far, near).wait_send()

    each(0, chunks, last_step)
    for t in range(tok):
        out[t] = wide_rows[t * micro:(t + 1) * micro, :]


def shards(sections, nodes, locals_, tokens, norm_gain, routes, gate_weight, w_gate, w_up, w_down):
    width, hid = w_gate.shape[1:]
    chunks = 7
    count = tokens.shape[0] * tokens.shape[1]
    group = locals_ * count
    total = nodes * group
    step = width // chunks
    pack, part = PIECES * count, step // PIECES
    bf, f32 = jnp.bfloat16, jnp.float32
    vmem, dma = pltpu.VMEM, pltpu.SemaphoreType.DMA
    here = pl.BlockSpec(memory_space=pltpu.VMEM)
    away = pl.BlockSpec(memory_space=pl.ANY)
    tokens = tokens.transpose(1, 0, 2)
    mixed = pl.pallas_call(
        functools.partial(kernel, sections, locals_, chunks),
        out_shape=jax.ShapeDtypeStruct(tokens.shape, f32),
        in_specs=[here] * 4 + [away] * 3,
        out_specs=here,
        scratch_shapes=[
            vmem((width, 2 * hid), bf), vmem((hid, width), bf),
            vmem((BLOCK, width), f32), vmem((chunks, pack, part), bf),
            vmem((chunks, locals_, pack, part), bf),
            vmem((nodes, group, width), bf),
            vmem((total, 2 * hid), f32),
            vmem(tokens.shape, bf),
            vmem((BLOCK, LANES), f32), vmem((nodes, locals_, BLOCK, LANES), f32),
            vmem((total + BLOCK, LANES), f32),
            vmem((locals_, pack + BLOCK, part), f32), vmem((group + BLOCK, step), f32),
            vmem((nodes, group, width), bf),
            vmem((2, group, width), bf),
            vmem((group, width), bf),
            vmem((chunks, locals_, pack, part), bf),
            vmem((chunks, locals_, pack, part), bf),
            dma((3, chunks)), dma, dma,
            dma((locals_,)), dma((locals_,)), dma((3,)), dma((3,)),
            dma((chunks, locals_)), dma((chunks, locals_)), dma((chunks, 3)), dma((chunks, 3)),
            dma((chunks, 2)), dma((chunks, 2)), dma((chunks,)), dma((chunks,)),
            dma((chunks, locals_)), dma((chunks, locals_)),
        ],
        compiler_params=pltpu.CompilerParams(
            collective_id=0, has_side_effects=True, vmem_limit_bytes=60 * 1024 * 1024
        ),
        cost_estimate=pl.CostEstimate(
            flops=6 * total * width * hid, bytes_accessed=6 * width * hid, transcendentals=total * hid
        ),
        name="expert_relay",
    )(
        tokens, norm_gain.reshape(1, width), routes.transpose(0, 2, 1), gate_weight.transpose(0, 2, 1),
        w_gate, w_up, w_down,
    )
    return mixed.astype(bf).transpose(1, 0, 2)


def solution(mesh):
    events = P(None, ("section", "node", "local"), None)
    sizes = (mesh.shape["section"], mesh.shape["node"], mesh.shape["local"])
    return jax.shard_map(
        functools.partial(shards, *sizes),
        mesh=mesh,
        in_specs=(events, P(), events, events, P("node", None, "local"), P("node", None, "local"), P("node", "local", None)),
        out_specs=events,
        check_vma=False,
    )
```

```python
import functools

import jax
import jax.numpy as jnp
from jax import lax
from jax.experimental import pallas as pl
from jax.experimental.pallas import tpu as pltpu
from jax.sharding import PartitionSpec as P

MESH = pl.DeviceIdType.MESH
BLOCK = 8
LANES = 128
FAR_LAG = 2
CORE_LAG = 2
PAIR_LAG = 4
PIECES = 4
AHEAD = 3


def kernel(
    sections, locals_, chunks,
    tokens, gain, routes, gate_weight, w_gate, w_up, w_down,
    out,
    both_v, down_v, wide_rows, packed, rows_in, rows, acts, arrived,
    own_weights, all_weights, row_weights, packing, spreading, parts, core_in, pair_in, sums, local_in,
    load_sem, a_send, a_recv, w1_send, w1_recv, w2_send, w2_recv,
    s1_send, s1_recv, s2_send, s2_recv, r1_send, r1_recv, r2_send, r2_recv, r3_send, r3_recv,
):
    tok, micro, width = tokens.shape
    hid = down_v.shape[0]
    step = width // chunks
    count = tok * micro
    group = locals_ * count
    total = rows.shape[0] * group
    part = step // PIECES
    pack = PIECES * count
    section, node, local = (lax.axis_index(name) for name in ("section", "node", "local"))
    ahead = lax.rem(section + 1, sections)
    behind = lax.rem(section + sections - 1, sections)
    near, far, cross = node ^ 1, node ^ 2, node ^ 3

    def cut(k):
        return pl.ds(pl.multiple_of(k * step, step), step)

    def narrow(k, p):
        return pl.ds(pl.multiple_of(k * step + p * part, part), part)

    def peer(offset):
        return lax.rem(local + offset, locals_)

    def each(first, last, body):
        lax.fori_loop(first, last, lambda k, c: (body(k), c)[1], 0)

    def send(src, dst, send_sem, recv_sem, to):
        return pltpu.make_async_remote_copy(
            src_ref=src, dst_ref=dst, send_sem=send_sem, recv_sem=recv_sem,
            device_id=to, device_id_type=MESH,
        )

    def gate_load(k):
        return pltpu.make_async_copy(w_gate.at[0, cut(k), :], both_v.at[cut(k), 0:hid], load_sem.at[0, k])

    def up_load(k):
        return pltpu.make_async_copy(w_up.at[0, cut(k), :], both_v.at[cut(k), hid:2 * hid], load_sem.at[1, k])

    def down_load(k):
        return pltpu.make_async_copy(w_down.at[0, :, cut(k)], down_v.at[:, cut(k)], load_sem.at[2, k])

    def start_in(k):
        gate_load(k).start()
        up_load(k).start()

    barrier = pltpu.get_barrier_semaphore()
    for other in range(locals_):
        pl.semaphore_signal(barrier, inc=1, device_id=(behind, node, other), device_id_type=MESH)
    for offset in range(1, locals_):
        pl.semaphore_signal(barrier, inc=1, device_id=(section, node, peer(offset)), device_id_type=MESH)
    for other in (near, far):
        pl.semaphore_signal(barrier, inc=1, device_id=(section, other, local), device_id_type=MESH)

    each(0, chunks, start_in)
    each(0, chunks, lambda k: down_load(k).start())

    own_weights[...] = jnp.zeros_like(own_weights)
    lane = lax.broadcasted_iota(jnp.int32, (routes.shape[1], LANES), 1)
    for t in range(tok):
        for m in range(micro):
            spread = jnp.where(routes[m, :, t:t + 1] == lane, gate_weight[m, :, t:t + 1], 0.0)
            own_weights[t * micro + m:t * micro + m + 1, :] = jnp.sum(spread, axis=0, keepdims=True)

    wide_rows[...] = jnp.zeros_like(wide_rows)
    for t in range(tok):
        wide = tokens[t].astype(jnp.float32)
        mean_square = jnp.mean(wide * wide, axis=1, keepdims=True)
        wide_rows[t * micro:(t + 1) * micro, :] = wide * lax.rsqrt(mean_square + 1e-06) * gain[...]
    packing[...] = jnp.zeros_like(packing)
    spreading[...] = jnp.zeros_like(spreading)

    def pack_own(k):
        for p in range(PIECES):
            packing[0, p * count:p * count + BLOCK, :] = wide_rows[:, narrow(k, p)]
        packed[k] = packing[0, 0:pack, :].astype(jnp.bfloat16)


    pl.semaphore_wait(barrier, 2 * locals_ + 1)

    def w_out(offset):
        return send(own_weights, all_weights.at[node, local], w1_send.at[offset], w1_recv.at[local],
                    (section, node, peer(offset)))

    for offset in range(1, locals_):
        w_out(offset).start()
    all_weights[node, local] = own_weights[...]

    def s1(k, offset):
        return send(packed.at[k], rows_in.at[k, local],
                    s1_send.at[k, offset], s1_recv.at[k, local], (ahead, node, peer(offset)))

    def s1_wait(k):
        for other in range(locals_):
            send(packed.at[k], rows_in.at[k, other],
                 s1_send.at[k, other], s1_recv.at[k, other], (ahead, node, local)).wait_recv()

    def s1_start(k):
        pack_own(k)
        for offset in range(locals_):
            s1(k, offset).start()

    each(0, AHEAD, s1_start)
    carry = send(tokens, arrived, a_send, a_recv, (ahead, node, local))

    def s2(k, which, block, to):
        return send(rows.at[block, :, cut(k)], rows.at[block, :, cut(k)],
                    s2_send.at[k, which], s2_recv.at[k, which], (section, to, local))

    acts[...] = jnp.zeros_like(acts)

    def w2(which, block, to):
        return send(all_weights.at[block], all_weights.at[block],
                    w2_send.at[which], w2_recv.at[which], (section, to, local))

    def in_step(i):
        @pl.when(i < chunks)
        def _():
            s1_wait(i)
            for other in range(locals_):
                packing[other, 0:pack, :] = rows_in[i, other].astype(jnp.float32)
                for p in range(PIECES):
                    spreading[other * count:other * count + BLOCK, p * part:(p + 1) * part] = (
                        packing[other, p * count:p * count + BLOCK, :]
                    )
            rows[node, :, cut(i)] = spreading[0:group, :].astype(jnp.bfloat16)
            s2(i, 0, node, far).start()
            s2(i, 1, node, near).start()

        @pl.when(i < chunks - AHEAD)
        def _():
            s1_start(i + AHEAD)

        @pl.when(i == chunks - 1)
        def _():
            carry.start()

        @pl.when(i == 1)
        def _():
            for other in range(1, locals_):
                source = peer(other)
                send(own_weights, all_weights.at[node, source], w1_send.at[other], w1_recv.at[source],
                     (section, node, source)).wait_recv()
            w2(0, node, far).start()
            w2(1, node, near).start()

        @pl.when(i == chunks)
        def _():
            w2(0, far, far).wait_recv()
            w2(2, far, near).start()

        @pl.when((i >= FAR_LAG) & (i < chunks + FAR_LAG))
        def _():
            k = i - FAR_LAG
            s2(k, 0, far, far).wait_recv()
            s2(k, 2, far, near).start()

        @pl.when(i > FAR_LAG)
        def _():
            k = i - FAR_LAG - 1
            s2(k, 1, near, near).wait_recv()
            s2(k, 2, cross, near).wait_recv()
            gate_load(k).wait()
            up_load(k).wait()
            piece = rows[:, :, cut(k)].astype(jnp.float32).reshape(total, step).astype(jnp.bfloat16)
            acts[...] += jnp.dot(piece, both_v[cut(k), :], preferred_element_type=jnp.float32)

    each(0, chunks + FAR_LAG + 1, in_step)

    gate = acts[:, 0:hid]
    hidden = (gate / (1.0 + jnp.exp(-gate)) * acts[:, hid:2 * hid]).astype(jnp.bfloat16)

    w2(1, near, near).wait_recv()
    w2(2, cross, near).wait_recv()
    for block in range(rows.shape[0]):
        for other in range(locals_):
            first = block * group + other * count
            row_weights[first:first + BLOCK, :] = all_weights[block, other]
    lanes = lax.broadcasted_iota(jnp.int32, (total, LANES), 1)
    weight = jnp.sum(jnp.where(lanes == node, row_weights[0:total, :], 0.0), axis=1, keepdims=True)

    def r1(k, which, block):
        return send(parts.at[block, :, cut(k)], core_in.at[which, :, cut(k)],
                    r1_send.at[k, which], r1_recv.at[k, which], (section, near, local))

    def r2(k):
        return send(parts.at[far, :, cut(k)], pair_in.at[:, cut(k)],
                    r2_send.at[k], r2_recv.at[k], (section, far, local))

    def r3(k, offset):
        return send(sums.at[k, peer(offset)], local_in.at[k, local],
                    r3_send.at[k, offset], r3_recv.at[k, local], (section, node, peer(offset)))

    def out_step(j):
        @pl.when(j == chunks)
        def _():
            carry.wait_recv()
            wide_rows[...] = jnp.zeros_like(wide_rows)
            for t in range(tok):
                wide_rows[t * micro:(t + 1) * micro, :] = arrived[t].astype(jnp.float32)

        @pl.when(j < chunks)
        def _():
            down_load(j).wait()
            term = jnp.dot(hidden, down_v[:, cut(j)], preferred_element_type=jnp.float32) * weight
            parts[:, :, cut(j)] = term.reshape(parts.shape[:2] + (step,)).astype(jnp.bfloat16)
            r1(j, 1, cross).start()
            r1(j, 0, near).start()
            for offset in range(locals_):
                s1(j, offset).wait_send()
            s2(j, 0, node, far).wait_send()
            s2(j, 1, node, near).wait_send()
            s2(j, 2, far, near).wait_send()

        @pl.when((j >= CORE_LAG) & (j < chunks + CORE_LAG))
        def _():
            k = j - CORE_LAG
            r1(k, 1, cross).wait_recv()
            r1(k, 0, near).wait_recv()
            both = parts[far, :, cut(k)].astype(jnp.float32) + core_in[1, :, cut(k)].astype(jnp.float32)
            parts[far, :, cut(k)] = both.astype(jnp.bfloat16)
            r2(k).start()

        @pl.when(j >= PAIR_LAG)
        def _():
            k = j - PAIR_LAG
            r2(k).wait_recv()
            spreading[0:group, :] = (
                parts[node, :, cut(k)].astype(jnp.float32)
                + core_in[0, :, cut(k)].astype(jnp.float32)
                + pair_in[:, cut(k)].astype(jnp.float32)
            )
            for other in range(locals_):
                for p in range(PIECES):
                    packing[other, p * count:p * count + BLOCK, :] = (
                        spreading[other * count:other * count + BLOCK, p * part:(p + 1) * part]
                    )
                sums[k, other] = packing[other, 0:pack, :].astype(jnp.bfloat16)
            for offset in range(1, locals_):
                r3(k, offset).start()

    def last_step(k):
        r1(k, 0, near).wait_send()
        r1(k, 1, cross).wait_send()
        r2(k).wait_send()
        for offset in range(1, locals_):
            r3(k, offset).wait_send()
        mixed = sums[k, local].astype(jnp.float32)
        for offset in range(1, locals_):
            source = peer(offset)
            send(sums.at[k, source], local_in.at[k, source],
                 r3_send.at[k, offset], r3_recv.at[k, source], (section, node, source)).wait_recv()
            mixed += local_in[k, source].astype(jnp.float32)
        packing[0, 0:pack, :] = mixed
        for p in range(PIECES):
            wide_rows[:, narrow(k, p)] += packing[0, p * count:p * count + BLOCK, :]

    each(0, chunks + PAIR_LAG, out_step)
    carry.wait_send()
    for offset in range(1, locals_):
        w_out(offset).wait_send()
    w2(0, node, far).wait_send()
    w2(1, node, near).wait_send()
    w2(2, far, near).wait_send()

    each(0, chunks, last_step)
    for t in range(tok):
        out[t] = wide_rows[t * micro:(t + 1) * micro, :]


def shards(sections, nodes, locals_, tokens, norm_gain, routes, gate_weight, w_gate, w_up, w_down):
    width, hid = w_gate.shape[1:]
    chunks = 7
    count = tokens.shape[0] * tokens.shape[1]
    group = locals_ * count
    total = nodes * group
    step = width // chunks
    pack, part = PIECES * count, step // PIECES
    bf, f32 = jnp.bfloat16, jnp.float32
    vmem, dma = pltpu.VMEM, pltpu.SemaphoreType.DMA
    here = pl.BlockSpec(memory_space=pltpu.VMEM)
    away = pl.BlockSpec(memory_space=pl.ANY)
    tokens = tokens.transpose(1, 0, 2)
    mixed = pl.pallas_call(
        functools.partial(kernel, sections, locals_, chunks),
        out_shape=jax.ShapeDtypeStruct(tokens.shape, f32),
        in_specs=[here] * 4 + [away] * 3,
        out_specs=here,
        scratch_shapes=[
            vmem((width, 2 * hid), bf), vmem((hid, width), bf),
            vmem((BLOCK, width), f32), vmem((chunks, pack, part), bf),
            vmem((chunks, locals_, pack, part), bf),
            vmem((nodes, group, width), bf),
            vmem((total, 2 * hid), f32),
            vmem(tokens.shape, bf),
            vmem((BLOCK, LANES), f32), vmem((nodes, locals_, BLOCK, LANES), f32),
            vmem((total + BLOCK, LANES), f32),
            vmem((locals_, pack + BLOCK, part), f32), vmem((group + BLOCK, step), f32),
            vmem((nodes, group, width), bf),
            vmem((2, group, width), bf),
            vmem((group, width), bf),
            vmem((chunks, locals_, pack, part), bf),
            vmem((chunks, locals_, pack, part), bf),
            dma((3, chunks)), dma, dma,
            dma((locals_,)), dma((locals_,)), dma((3,)), dma((3,)),
            dma((chunks, locals_)), dma((chunks, locals_)), dma((chunks, 3)), dma((chunks, 3)),
            dma((chunks, 2)), dma((chunks, 2)), dma((chunks,)), dma((chunks,)),
            dma((chunks, locals_)), dma((chunks, locals_)),
        ],
        compiler_params=pltpu.CompilerParams(
            collective_id=0, has_side_effects=True, vmem_limit_bytes=60 * 1024 * 1024
        ),
        cost_estimate=pl.CostEstimate(
            flops=6 * total * width * hid, bytes_accessed=6 * width * hid, transcendentals=total * hid
        ),
        name="expert_relay",
    )(
        tokens, norm_gain.reshape(1, width), routes.transpose(0, 2, 1), gate_weight.transpose(0, 2, 1),
        w_gate, w_up, w_down,
    )
    return mixed.astype(bf).transpose(1, 0, 2)


def solution(mesh):
    events = P(None, ("section", "node", "local"), None)
    sizes = (mesh.shape["section"], mesh.shape["node"], mesh.shape["local"])
    return jax.shard_map(
        functools.partial(shards, *sizes),
        mesh=mesh,
        in_specs=(events, P(), events, events, P("node", None, "local"), P("node", None, "local"), P("node", "local", None)),
        out_specs=events,
        check_vma=False,
    )
```
